512 devices in a mesh: seq: 64 (over z_hi, y, x, core), tp: 8 (over z_lo).
Axes of the slice: x: 4, y: 4, z: 16 (z_hi: 2, z_lo: 8; z = z_hi * 8 + z_lo), core: 2. Of those that a mesh axis runs over, the one named last changes fastest.
Arguments:
- projected: bfloat16 [3, 65536, 4096], P(None, 'seq', 'tp'), may hold values from -6 to 6
- short_taps: float32 [3, 3, 4096], P(None, None, 'tp'), may hold values from -3 to 3
- long_filter: bfloat16 [256, 128], P('tp'), may hold values from -0.5 to 0.5
- out_weight: bfloat16 [4096, 4096], P('seq', 'tp'), may hold values from -0.09375 to 0.09375
Outputs:
- mixed: bfloat16 [65536, 4096], P('seq', 'tp')
The draws below stay inside these ranges and needn't reach their ends.
All inputs are finite; a program needn't handle non-finite values.
Results may differ from the reference program's by a relative error of at most 0.0057.
Values may be sent and summed in bfloat16 or wider, within the bound.
No kernel may reach another device: no remote copies, remote signals or barrier semaphores. Data moves between devices by JAX's collectives and lax.ppermute only.
A program may use at most 64 MiB of HBM per device.

```python
import jax
import jax.numpy as jnp
from jax import lax

D = 4096
TAPS = 128
TOKENS = 65536
GROUPS = 256


def levels(own_key, shape, cuts, low, largest):
    gain = 1.0
    for dim, shards_of in cuts:
        steps = jax.random.uniform(jax.random.fold_in(jax.random.fold_in(own_key, 6), dim), (shards_of,), jnp.float32, low / len(cuts), largest / len(cuts))
        gain = gain * jnp.repeat(jnp.exp(steps), shape[dim] // shards_of).reshape((-1,) + (1,) * (len(shape) - 1 - dim))
    return gain


def normal_values(own_key, dims, scale, most, cuts=(), kind=jnp.bfloat16):
    array = jax.random.normal(own_key, dims, jnp.float32) * scale
    if len(cuts) > 0:
        array = levels(own_key, dims, cuts, -0.22, 0.18) * array
    return jnp.clip(array, min=-most, max=most).astype(kind)


def setup_inputs(seed: int = 0) -> dict:
    keys = jax.random.split(jax.random.key(seed), 5)
    return {
        "projected": normal_values(keys[0], (3, TOKENS, D), 1.0, 6.0, ((1, 64), (2, 8))),
        "short_taps": normal_values(keys[1], (3, 3, D), 0.6, 3.0, ((2, 8),), jnp.float32),
        "long_filter": normal_values(keys[2], (GROUPS, TAPS), 0.09, 0.5, ((0, 8),)),
        "out_weight": normal_values(keys[3], (D, D), D ** -0.5, 0.09375, ((0, 64), (1, 8))),
    }


def toeplitz_blocks(long_filter):
    groups, taps = long_filter.shape
    reverse = long_filter[:, ::-1]
    zeros_pad = jnp.zeros((groups, taps), long_filter.dtype)
    padded = jnp.concatenate([zeros_pad, reverse, zeros_pad], axis=1)
    rows_idx = jnp.arange(taps, dtype=jnp.int32)[:, None]
    cols_idx = jnp.arange(2 * taps, dtype=jnp.int32)[None, :]
    return jnp.take(padded, cols_idx - rows_idx + taps, axis=1)


def reference(projected, short_taps, long_filter, out_weight):
    taps = long_filter.shape[1]
    groups = long_filter.shape[0]
    width = projected.shape[2]
    length = projected.shape[1]
    block = 512
    padded = jnp.pad(projected, ((0, 0), (taps + 1, 0), (0, 0)))
    toeplitz = toeplitz_blocks(long_filter).astype(jnp.float32)
    tap_zero = short_taps[:, 0][:, None, :]
    tap_one = short_taps[:, 1][:, None, :]
    tap_two = short_taps[:, 2][:, None, :]

    def one_block(index):
        start = (index * block).astype(jnp.int32)
        raw = lax.dynamic_slice(padded, (jnp.int32(0), start, jnp.int32(0)), (3, block + taps + 1, width))
        feat = tap_zero * raw[:, 2:] + tap_one * raw[:, 1:-1] + tap_two * raw[:, :-2]
        query_feat = feat[0, taps - 1:]
        gated_in = (feat[1] * feat[2]).astype(jnp.bfloat16)
        gated_pad = jnp.concatenate([gated_in, jnp.zeros((1, width), jnp.bfloat16)], axis=0)
        pieces = gated_pad.reshape(block // taps + 1, taps, width)
        windows = jnp.concatenate([pieces[:-1], pieces[1:]], axis=1)
        windows = windows.reshape(block // taps, 2 * taps, groups, width // groups).astype(jnp.float32)
        conv = jnp.einsum("gab,nbgc->nagc", toeplitz, windows).reshape(block, width)
        gated_out = (query_feat * conv).astype(jnp.bfloat16)
        return jnp.dot(gated_out, out_weight, preferred_element_type=jnp.float32).astype(jnp.bfloat16)

    result = lax.map(one_block, jnp.arange(length // block, dtype=jnp.int32))
    return result.reshape(length, width)
```

```python
import functools

import jax
import jax.numpy as jnp
from jax import lax
from jax.experimental import pallas as pl
from jax.experimental.pallas import tpu as pltpu
from jax.sharding import Mesh, PartitionSpec as P

SEQ = ("zh", "y", "x", "c")
PLANE = ("y", "x", "c")
LINE = ("c", "tp")
HALO = 144
LANES = 128
LINE_LEN = 8
WORKERS = 4


def on_line(pairs):
    place = lambda u, core: core * LINE_LEN + (u if core == 0 else LINE_LEN - 1 - u)
    return [(place(a, core), place(b, core)) for core in (0, 1) for a, b in pairs]


def inward(block, step):
    return lax.ppermute(block, LINE, on_line([(u, u - 1) for u in range(1, LINE_LEN + 1 - step)]))


def outward(block, step):
    return lax.ppermute(block, LINE, on_line([(u, u + 1) for u in range(step - 1, WORKERS - 1)]))


def deliver(block, workers):
    return lax.ppermute(block, LINE, on_line([(u, u + WORKERS) for u in workers]))


def feature(rows, taps):
    return (
        taps[0:1] * rows
        + taps[1:2] * pltpu.roll(rows, 1, 0)
        + taps[2:3] * pltpu.roll(rows, 2, 0)
    )


def local_kernel(early, x_ref, halo_ref, taps_ref, filt_ref, out_ref, toep):
    groups, taps = filt_ref.shape[1], filt_ref.shape[2]
    half = out_ref.shape[0]
    width = LANES // groups
    lag = lax.broadcasted_iota(jnp.int32, (taps, 2 * taps), 0)
    col = lax.broadcasted_iota(jnp.int32, (taps, 2 * taps), 1)
    flip = jnp.where(lag + col == taps, 1.0, 0.0).astype(jnp.bfloat16)
    first = jnp.dot(filt_ref[0], flip, preferred_element_type=jnp.float32)
    for g in range(groups):
        wide = jnp.broadcast_to(first[g : g + 1], (taps, 2 * taps))
        wide = pltpu.roll(wide, 0, 1, stride=1, stride_axis=0)
        toep[g * taps : (g + 1) * taps] = wide.astype(jnp.bfloat16)

    def rows(stream):
        if early:
            own = x_ref[stream, :half].astype(jnp.float32)
            return jnp.concatenate([halo_ref[stream].astype(jnp.float32), own], axis=0)
        return x_ref[stream, half - HALO :].astype(jnp.float32)

    query = feature(rows(0), taps_ref[0])[HALO:]
    gated = feature(rows(1), taps_ref[1]) * feature(rows(2), taps_ref[2])
    gated = gated[HALO - taps :].astype(jnp.bfloat16)
    group_of = lax.broadcasted_iota(jnp.int32, (taps, 2 * LANES), 1) % LANES // width
    for pair in range(half // taps // 2):
        base = 2 * pair * taps
        window = jnp.concatenate(
            [gated[base : base + 2 * taps], gated[base + taps : base + 3 * taps]], axis=1
        )
        every = jnp.dot(toep[...], window, preferred_element_type=jnp.float32)
        conv = every[:taps]
        for g in range(1, groups):
            conv = jnp.where(group_of == g, every[g * taps : (g + 1) * taps], conv)
        for k in range(2):
            at = base + k * taps
            piece = conv[:, k * LANES : (k + 1) * LANES] * query[at : at + taps]
            out_ref[at : at + taps] = piece.astype(jnp.bfloat16)


def local_part(early, x, halo, short_taps, long_filter):
    streams, tokens, channels = x.shape
    groups, taps = long_filter.shape
    tiles = channels // LANES
    filt = long_filter.reshape(tiles, groups // tiles, taps)
    half = tokens // 2
    return pl.pallas_call(
        functools.partial(local_kernel, early),
        grid=(tiles,),
        in_specs=[
            pl.BlockSpec((streams, tokens, LANES), lambda i: (0, 0, i)),
            pl.BlockSpec((streams, HALO, LANES), lambda i: (0, 0, i)),
            pl.BlockSpec((streams, 3, LANES), lambda i: (0, 0, i)),
            pl.BlockSpec((1, groups // tiles, taps), lambda i: (i, 0, 0)),
        ],
        out_specs=pl.BlockSpec((half, LANES), lambda i: (0, i)),
        out_shape=jax.ShapeDtypeStruct((half, channels), jnp.bfloat16),
        scratch_shapes=[pltpu.VMEM((groups // tiles * taps, 2 * taps), jnp.bfloat16)],
        compiler_params=pltpu.CompilerParams(vmem_limit_bytes=32 << 20),
        cost_estimate=pl.CostEstimate(flops=1 << 30, bytes_accessed=4 << 20, transcendentals=0),
        name="early_tokens" if early else "late_tokens",
    )(x, halo, short_taps, filt)


def project_kernel(blocks, has_start, y_ref, z_ref, *refs):
    x_refs, w_ref = refs[: 2 * blocks], refs[2 * blocks]
    start_ref = refs[2 * blocks + 1] if has_start else None
    out_ref, acc = refs[-2:]
    step = pl.program_id(0)
    depth = x_refs[0].shape[1]
    half = x_refs[0].shape[0]
    weight = w_ref[...].reshape(depth, w_ref.shape[-1])
    for i in range(blocks):

        @pl.when(step == i)
        def _():
            for part in range(2):
                at = pl.ds(part * half, half)
                term = jnp.dot(
                    x_refs[2 * i + part][...], weight, preferred_element_type=jnp.float32
                )
                if i == 0 and has_start:
                    term = start_ref[at] + term
                elif i > 0:
                    term = acc[at] + term
                if i == blocks - 1:
                    out_ref[at] = term.astype(out_ref.dtype)
                else:
                    acc[at] = term


def project(pairs, index, weights, side, start, kind, name):
    blocks = len(pairs)
    half, depth = pairs[0][0].shape
    ys, members, zs, rows, columns = weights.shape
    columns //= 2
    whole = lambda i, y, z: (0, 0)
    in_specs = [pl.BlockSpec((half, depth), whole)] * (2 * blocks)
    in_specs.append(
        pl.BlockSpec((1, members, 1, rows, columns), lambda i, y, z: (y[i], 0, z[i], 0, side))
    )
    operands = [part for pair in pairs for part in pair] + [weights]
    if start is not None:
        in_specs.append(pl.BlockSpec((2 * half, columns), whole))
        operands.append(start)
    return pl.pallas_call(
        functools.partial(project_kernel, blocks, start is not None),
        grid_spec=pltpu.PrefetchScalarGridSpec(
            num_scalar_prefetch=2,
            grid=(blocks,),
            in_specs=in_specs,
            out_specs=pl.BlockSpec((2 * half, columns), whole),
            scratch_shapes=[pltpu.VMEM((2 * half, columns), jnp.float32)],
        ),
        out_shape=jax.ShapeDtypeStruct((2 * half, columns), kind),
        compiler_params=pltpu.CompilerParams(vmem_limit_bytes=48 << 20),
        cost_estimate=pl.CostEstimate(
            flops=4 * blocks * half * depth * columns,
            bytes_accessed=blocks * 2 * (2 * half * depth + depth * columns),
            transcendentals=0,
        ),
        name=name,
    )(index[0], index[1], *operands)


def per_device(projected, short_taps, long_filter, out_weight):
    streams, tokens, channels = projected.shape
    core, at, zh = lax.axis_index("c"), lax.axis_index("tp"), lax.axis_index("zh")
    u = jnp.where(core == 0, at, LINE_LEN - 1 - at)
    toward = jnp.where(core == 0, 1, -1)
    others = lambda hop: [(i, (i + hop) % LINE_LEN) for i in range(LINE_LEN)]
    swap_zh = [(0, 1), (1, 0)]

    far = lax.ppermute(out_weight, "zh", swap_zh)
    next_seq = [(i, i + 1) for i in range(lax.axis_size(SEQ) - 1)]
    halo = lax.ppermute(projected[:, tokens - HALO :], SEQ, next_seq)
    near_partner = lax.ppermute(out_weight, "tp", others(WORKERS))
    both = lambda z, t: z * LINE_LEN + t
    far_partner = lax.ppermute(
        out_weight,
        ("zh", "tp"),
        [(both(z, t), both(1 - z, (t + WORKERS) % LINE_LEN)) for z in (0, 1) for t in range(LINE_LEN)],
    )
    shard = jnp.concatenate(
        [
            jnp.concatenate([out_weight, near_partner], axis=1),
            jnp.concatenate([far, far_partner], axis=1),
        ],
        axis=0,
    )
    weights = lax.all_gather(shard, PLANE, axis=0, tiled=True)
    rows, columns = out_weight.shape
    weights = weights.reshape(lax.axis_size("y"), -1, 2, rows, 2 * columns)

    def rows_of(distances):
        block = jnp.stack([jnp.clip(at + toward * d, 0, LINE_LEN - 1) for d in distances])
        per_zh = lax.axis_size("y")
        return (block % per_zh).astype(jnp.int32), (block // per_zh != zh).astype(jnp.int32)

    late = local_part(False, projected, projected[:, :HALO], short_taps, long_filter)
    early = local_part(True, projected, halo, short_taps, long_filter)
    own = (early, late)

    came = [own]
    for step in range(1, LINE_LEN):
        before, behind = came[-1]
        behind = inward(behind, step)
        before = inward(before, step)
        came.append((before, behind))
    back = [own]
    for step in range(1, WORKERS):
        before, behind = back[-1]
        back.append((outward(before, step), outward(behind, step)))

    pick = lambda yes, one, other: tuple(jnp.where(yes, a, b) for a, b in zip(one, other))
    fifth = pick(u < WORKERS - 1, came[5], back[3])
    fifth_at = jnp.where(u < WORKERS - 1, 5, -3)
    first_blocks = came[:5] + [fifth, back[1], back[2]]
    first_index = rows_of([0, 1, 2, 3, 4, fifth_at, -1, -2])
    total = project(first_blocks, first_index, weights, 1, None, jnp.float32, "partner_first")
    sent_two = deliver(total.astype(jnp.bfloat16), (2, 3))
    total = project([came[6]], rows_of([6]), weights, 1, total, jnp.float32, "partner_sixth")
    sent_one = deliver(total.astype(jnp.bfloat16), (1,))
    total = project([came[7]], rows_of([7]), weights, 1, total, jnp.bfloat16, "partner_last")
    sent_last = deliver(total, (0,))

    sixth = pick(u < WORKERS - 2, came[6], back[2])
    sixth_at = jnp.where(u < WORKERS - 2, 6, -2)
    seventh = pick(u < WORKERS - 3, came[7], back[1])
    seventh_at = jnp.where(u < WORKERS - 3, 7, -1)
    own_blocks = came[:5] + [fifth, sixth, seventh]
    own_index = rows_of([0, 1, 2, 3, 4, fifth_at, sixth_at, seventh_at])
    mine = project(own_blocks, own_index, weights, 0, None, jnp.bfloat16, "own_columns")
    given = jnp.where(u == WORKERS, sent_last, jnp.where(u == WORKERS + 1, sent_one, sent_two))
    return jnp.where(u < WORKERS, mine, given)


def solution(mesh):
    split = Mesh(mesh.devices.reshape(2, 4, 4, 2, LINE_LEN), ("zh", "y", "x", "c", "tp"))
    in_specs = (P(None, SEQ, "tp"), P(None, None, "tp"), P("tp", None), P(SEQ, "tp"))
    return jax.shard_map(
        per_device, mesh=split, in_specs=in_specs, out_specs=P(SEQ, "tp"), check_vma=False
    )
```

```python
import functools

import jax
import jax.numpy as jnp
from jax import lax
from jax.experimental import pallas as pl
from jax.experimental.pallas import tpu as pltpu
from jax.sharding import Mesh, PartitionSpec as P

SEQ = ("zh", "y", "x", "c")
PLANE = ("y", "x", "c")
TP = ("th", "tl")
LINE = ("c",) + TP
LANES = 128
LINE_LEN = 8
WORKERS = 4
VMEM = 60 << 20


def on_line(pairs):
    place = lambda u, core: core * LINE_LEN + (u if core == 0 else LINE_LEN - 1 - u)
    return [(place(a, core), place(b, core)) for core in (0, 1) for a, b in pairs]


def inward(block, step):
    return lax.ppermute(block, LINE, on_line([(u, u - 1) for u in range(1, LINE_LEN + 1 - step)]))


def outward(block, step):
    return lax.ppermute(block, LINE, on_line([(u, u + 1) for u in range(step - 1, WORKERS - 1)]))


def deliver(block, workers):
    return lax.ppermute(block, LINE, on_line([(u, u + WORKERS) for u in workers]))


def feature(rows, taps):
    return (
        taps[0:1] * rows
        + taps[1:2] * pltpu.roll(rows, 1, 0)
        + taps[2:3] * pltpu.roll(rows, 2, 0)
    )


def toeplitz(filt_ref, toep):
    groups, taps = filt_ref.shape[1], filt_ref.shape[2]
    lag = lax.broadcasted_iota(jnp.int32, (taps, 2 * taps), 0)
    col = lax.broadcasted_iota(jnp.int32, (taps, 2 * taps), 1)
    flip = jnp.where(lag + col == taps, 1.0, 0.0).astype(jnp.bfloat16)
    first = jnp.dot(filt_ref[0], flip, preferred_element_type=jnp.float32)
    for g in range(groups):
        wide = jnp.broadcast_to(first[g : g + 1], (taps, 2 * taps))
        wide = pltpu.roll(wide, 0, 1, stride=1, stride_axis=0)
        toep[g * taps : (g + 1) * taps] = wide.astype(jnp.bfloat16)


def convolve(gated, query, groups, taps, toep, out_ref):
    group_of = lax.broadcasted_iota(jnp.int32, (taps, 2 * LANES), 1) % LANES // (LANES // groups)
    for pair in range(query.shape[0] // taps // 2):
        base = 2 * pair * taps
        window = jnp.concatenate(
            [gated[base : base + 2 * taps], gated[base + taps : base + 3 * taps]], axis=1
        )
        every = jnp.dot(toep[...], window, preferred_element_type=jnp.float32)
        conv = every[:taps]
        for g in range(1, groups):
            conv = jnp.where(group_of == g, every[g * taps : (g + 1) * taps], conv)
        for k in range(2):
            at = base + k * taps
            piece = conv[:, k * LANES : (k + 1) * LANES] * query[at : at + taps]
            out_ref[at : at + taps] = piece.astype(jnp.bfloat16)


def tail_kernel(x_ref, taps_ref, tail_ref):
    taps = tail_ref.shape[0] - 32
    rows = [x_ref[s, x_ref.shape[1] - taps - 16 :].astype(jnp.float32) for s in range(3)]
    gated = feature(rows[1], taps_ref[1]) * feature(rows[2], taps_ref[2])
    raw = [r[taps + 8 :] for r in rows]
    raw.append(jnp.zeros((8, LANES), jnp.float32))
    tail_ref[:taps] = gated[16:].astype(jnp.bfloat16)
    tail_ref[taps:] = jnp.concatenate(raw, axis=0).astype(jnp.bfloat16)


def late_kernel(x_ref, taps_ref, filt_ref, out_ref, toep):
    groups, taps = filt_ref.shape[1], filt_ref.shape[2]
    toeplitz(filt_ref, toep)
    rows = [x_ref[s, out_ref.shape[0] - taps - 16 :].astype(jnp.float32) for s in range(3)]
    query = feature(rows[0], taps_ref[0])[taps + 16 :]
    gated = feature(rows[1], taps_ref[1]) * feature(rows[2], taps_ref[2])
    convolve(gated[16:].astype(jnp.bfloat16), query, groups, taps, toep, out_ref)


def early_kernel(x_ref, halo_ref, taps_ref, filt_ref, out_ref, toep):
    groups, taps = filt_ref.shape[1], filt_ref.shape[2]
    half = out_ref.shape[0]
    toeplitz(filt_ref, toep)
    before = halo_ref[taps:].astype(jnp.float32)

    def featured(s):
        own = x_ref[s, :half].astype(jnp.float32)
        rows = jnp.concatenate([before[8 * s : 8 * s + 8], own], axis=0)
        return feature(rows, taps_ref[s])[8:]

    gated = (featured(1) * featured(2)).astype(jnp.bfloat16)
    gated = jnp.concatenate([halo_ref[:taps], gated], axis=0)
    convolve(gated, featured(0), groups, taps, toep, out_ref)


def lane_tiles(rows):
    return pl.BlockSpec((rows, LANES), lambda i: (0, i))


LOCAL = dict(
    compiler_params=pltpu.CompilerParams(vmem_limit_bytes=VMEM),
    cost_estimate=pl.CostEstimate(flops=1 << 30, bytes_accessed=4 << 20, transcendentals=0),
)


def local_tail(x, short_taps, taps):
    streams, tokens, channels = x.shape
    last = 2 * taps
    return pl.pallas_call(
        tail_kernel,
        grid=(channels // LANES,),
        in_specs=[
            pl.BlockSpec((streams, last, LANES), lambda i: (0, tokens // last - 1, i)),
            pl.BlockSpec((streams, 3, LANES), lambda i: (0, 0, i)),
        ],
        out_specs=lane_tiles(taps + 32),
        out_shape=jax.ShapeDtypeStruct((taps + 32, channels), jnp.bfloat16),
        name="tail_tokens",
        **LOCAL,
    )(x, short_taps)


def local_part(x, halo, short_taps, long_filter):
    streams, tokens, channels = x.shape
    groups, taps = long_filter.shape
    tiles = channels // LANES
    filt = long_filter.reshape(tiles, groups // tiles, taps)
    in_specs = [
        pl.BlockSpec((streams, tokens, LANES), lambda i: (0, 0, i)),
        pl.BlockSpec((streams, 3, LANES), lambda i: (0, 0, i)),
        pl.BlockSpec((1, groups // tiles, taps), lambda i: (i, 0, 0)),
    ]
    operands = [x, short_taps, filt]
    if halo is not None:
        in_specs.insert(1, lane_tiles(halo.shape[0]))
        operands.insert(1, halo)
    return pl.pallas_call(
        late_kernel if halo is None else early_kernel,
        grid=(tiles,),
        in_specs=in_specs,
        out_specs=lane_tiles(tokens // 2),
        out_shape=jax.ShapeDtypeStruct((tokens // 2, channels), jnp.bfloat16),
        scratch_shapes=[pltpu.VMEM((groups // tiles * taps, 2 * taps), jnp.bfloat16)],
        name="late_tokens" if halo is None else "early_tokens",
        **LOCAL,
    )(*operands)


def project_kernel(slots, side, outs, has_start, place_ref, *refs):
    total = sum(count for _, options in slots for _, count in options)
    x_refs, w_ref = refs[:total], refs[total]
    held, weight, acc, x_sems, w_sems, start_sem = refs[-6:]
    out_refs = refs[len(refs) - 6 - outs : len(refs) - 6]
    at, toward, th, u = [place_ref[i] for i in range(4)]
    parts, half, depth = held.shape[1:]
    per_zh = w_ref.shape[0]

    def fetch(slot, first, count, part):
        source = x_refs[first + part] if count > 1 else x_refs[first].at[pl.ds(part * half, half)]
        return pltpu.make_async_copy(source, held.at[slot, part], x_sems.at[slot, part])

    def rows(slot, y, z):
        return pltpu.make_async_copy(w_ref.at[y, :, z], weight.at[slot], w_sems.at[slot])

    firsts = []
    position = 0
    for slot, (limit, options) in enumerate(slots):
        distance = options[0][0]
        if limit is not None:
            distance = jnp.where(u < limit, distance, options[1][0])
        block = jnp.clip(at + toward * distance, 0, LINE_LEN - 1)
        upper = jnp.where(block >= per_zh, 1, 0)
        column = th if side == 0 else 1 - th
        rows(slot, block - per_zh * upper, 2 * upper + column).start()
        firsts.append((position, options[0][1]))
        for option, (_, count) in enumerate(options):
            for part in range(parts):
                copy = fetch(slot, position, count, part)
                if limit is None:
                    copy.start()
                else:
                    pl.when(u < limit if option == 0 else u >= limit)(copy.start)
            position += count
    if has_start:
        from_start = pltpu.make_async_copy(refs[total + 1], acc, start_sem)
        from_start.start()
        from_start.wait()

    for slot in range(len(slots)):
        rows(slot, 0, 0).wait()
        for part in range(parts):
            fetch(slot, *firsts[slot], part).wait()
        term = jnp.dot(
            held[slot].reshape(parts * half, depth),
            weight[slot].reshape(depth, weight.shape[-1]),
            preferred_element_type=jnp.float32,
        )
        if slot > 0 or has_start:
            term = acc[...] + term
        if slot < len(slots) - 1:
            acc[...] = term
        else:
            for out_ref in out_refs:
                out_ref[...] = term.astype(out_ref.dtype)


def project(slots, place, weights, side, start, kinds, name):
    half, depth = slots[0][1][0][1][0].shape
    ys, members, zs, rows, columns = weights.shape
    blocks, tokens = len(slots), 2 * half
    operands = [part for _, options in slots for _, block in options for part in block] + [weights]
    if start is not None:
        operands.append(start)
    shape_of_slots = tuple(
        (limit, tuple((distance, len(block)) for distance, block in options)) for limit, options in slots
    )
    return pl.pallas_call(
        functools.partial(project_kernel, shape_of_slots, side, len(kinds), start is not None),
        grid_spec=pltpu.PrefetchScalarGridSpec(
            num_scalar_prefetch=1,
            grid=(1,),
            in_specs=[pl.BlockSpec(memory_space=pl.ANY)] * len(operands),
            out_specs=[pl.BlockSpec((tokens, columns), lambda i, place: (0, 0))] * len(kinds),
            scratch_shapes=[
                pltpu.VMEM((blocks, 2, half, depth), jnp.bfloat16),
                pltpu.VMEM((blocks, members, rows, columns), jnp.bfloat16),
                pltpu.VMEM((tokens, columns), jnp.float32),
                pltpu.SemaphoreType.DMA((blocks, 2)),
                pltpu.SemaphoreType.DMA((blocks,)),
                pltpu.SemaphoreType.DMA,
            ],
        ),
        out_shape=[jax.ShapeDtypeStruct((tokens, columns), kind) for kind in kinds],
        compiler_params=pltpu.CompilerParams(vmem_limit_bytes=VMEM),
        cost_estimate=pl.CostEstimate(
            flops=tokens * columns, bytes_accessed=tokens * columns, transcendentals=0
        ),
        name=name,
    )(place, *operands)


def per_device(projected, short_taps, long_filter, out_weight):
    core, at, th = lax.axis_index("c"), lax.axis_index(TP), lax.axis_index("th")
    u = jnp.where(core == 0, at, LINE_LEN - 1 - at)
    toward = jnp.where(core == 0, 1, -1)
    place = jnp.stack([at, toward, th, u]).astype(jnp.int32)
    in_order = lax.optimization_barrier

    tail = local_tail(projected, short_taps, long_filter.shape[1])
    next_seq = [(i, i + 1) for i in range(lax.axis_size(SEQ) - 1)]
    halo = lax.ppermute(tail, SEQ, next_seq)

    projected, place, _ = in_order((projected, place, tail))
    late = local_part(projected, None, short_taps, long_filter)

    own_shard, _ = in_order((out_weight, late))
    shard = lax.all_gather(own_shard, ("zh", "th"), axis=0, tiled=True)
    projected, halo, shard = in_order((projected, halo, shard))
    weights = lax.all_gather(shard, PLANE, axis=0, tiled=True)
    projected, halo, _ = in_order((projected, halo, shard))
    early = local_part(projected, halo, short_taps, long_filter)
    rows, columns = out_weight.shape
    parts = lax.axis_size(("zh", "th"))
    weights = weights.reshape(lax.axis_size("y"), -1, parts, rows, columns)

    came = [(early, late)]
    back = [(early, late)]
    for step in range(1, LINE_LEN - 2):
        before, behind = came[-1]
        before = inward(before, step)
        behind = inward(behind, step)
        came.append((before, behind))
        if step > 2:
            back.append(tuple(outward(part, step - 2) for part in back[-1]))

    kinds = (jnp.float32, jnp.bfloat16)
    near = [(None, [(d, came[d])]) for d in range(5)]
    (total,) = project(near, place, weights, 1, None, kinds[:1], "partner_near")
    fifth = came[5]
    came.append(tuple(inward(part, LINE_LEN - 2) for part in fifth))
    sixth, total = in_order((came[6], total))
    came.append(tuple(inward(part, LINE_LEN - 1) for part in sixth))
    far = [(3, [(5, fifth), (-3, back[3])]), (None, [(-2, back[2])]), (None, [(-1, back[1])])]
    total, ready = project(far, place, weights, 1, total, kinds, "partner_far")
    sent_two = deliver(ready, (2, 3))
    last, total = in_order((came[7], total))
    end = [(None, [(6, sixth)]), (None, [(7, last)])]
    (ready,) = project(end, place, weights, 1, total, kinds[1:], "partner_last")
    sent_last = deliver(ready, (0, 1))

    every = near + far[:1] + [(2, [(6, sixth), (-2, back[2])]), (1, [(7, last), (-1, back[1])])]
    (mine,) = project(every, place, weights, 0, None, kinds[1:], "own_columns")
    given = jnp.where(u < WORKERS + 2, sent_last, sent_two)
    return jnp.where(u < WORKERS, mine, given)


def solution(mesh):
    split = Mesh(mesh.devices.reshape(2, 4, 4, 2, 2, WORKERS), SEQ + TP)
    in_specs = (P(None, SEQ, TP), P(None, None, TP), P(TP, None), P(SEQ, TP))
    return jax.shard_map(
        per_device, mesh=split, in_specs=in_specs, out_specs=P(SEQ, TP), check_vma=False
    )
```

```python
import functools

import jax
import jax.numpy as jnp
from jax import lax
from jax.experimental import pallas as pl
from jax.experimental.pallas import tpu as pltpu
from jax.sharding import Mesh, PartitionSpec as P

SEQ = ("zh", "y", "x", "c")
PLANE = ("y", "x", "c")
TP = ("th", "tl")
LINE = ("c",) + TP
LANES = 128
LINE_LEN = 8
WORKERS = 4
VMEM = 60 << 20


def on_line(pairs):
    place = lambda u, core: core * LINE_LEN + (u if core == 0 else LINE_LEN - 1 - u)
    return [(place(a, core), place(b, core)) for core in (0, 1) for a, b in pairs]


def inward(block, step):
    return lax.ppermute(block, LINE, on_line([(u, u - 1) for u in range(1, LINE_LEN + 1 - step)]))


def outward(block, step):
    return lax.ppermute(block, LINE, on_line([(u, u + 1) for u in range(step - 1, WORKERS - 1)]))


def deliver(block, workers):
    return lax.ppermute(block, LINE, on_line([(u, u + WORKERS) for u in workers]))


def feature(rows, taps):
    return (
        taps[0:1] * rows
        + taps[1:2] * pltpu.roll(rows, 1, 0)
        + taps[2:3] * pltpu.roll(rows, 2, 0)
    )


def toeplitz(filt, toep):
    groups, taps = filt.shape
    lag = lax.broadcasted_iota(jnp.int32, (taps, 2 * taps), 0)
    col = lax.broadcasted_iota(jnp.int32, (taps, 2 * taps), 1)
    flip = jnp.where(lag + col == taps, 1.0, 0.0).astype(jnp.bfloat16)
    first = jnp.dot(filt, flip, preferred_element_type=jnp.float32)
    for g in range(groups):
        wide = jnp.broadcast_to(first[g : g + 1], (taps, 2 * taps))
        wide = pltpu.roll(wide, 0, 1, stride=1, stride_axis=0)
        toep[g * taps : (g + 1) * taps] = wide.astype(jnp.bfloat16)


def convolve(gated, query, groups, taps, toep):
    group_of = lax.broadcasted_iota(jnp.int32, (taps, 2 * LANES), 1) % LANES // (LANES // groups)
    pieces = []
    for pair in range(query.shape[0] // taps // 2):
        base = 2 * pair * taps
        window = jnp.concatenate(
            [gated[base : base + 2 * taps], gated[base + taps : base + 3 * taps]], axis=1
        )
        every = jnp.dot(toep[...], window, preferred_element_type=jnp.float32)
        conv = every[:taps]
        for g in range(1, groups):
            conv = jnp.where(group_of == g, every[g * taps : (g + 1) * taps], conv)
        for k in range(2):
            at = base + k * taps
            piece = conv[:, k * LANES : (k + 1) * LANES] * query[at : at + taps]
            pieces.append(piece.astype(jnp.bfloat16))
    return pieces


def local_kernel(late, x_ref, taps_ref, filt_ref, halo_ref, *refs):
    out_ref, tail_ref = refs[0], refs[1] if late else None
    rows_ref, taps_held, filt_held, halo_held, toep, sems = refs[-6:]
    streams, count = rows_ref.shape[:2]
    tiles, groups, taps = filt_held.shape
    first = x_ref.shape[1] - count if late else 0
    copies = [pltpu.make_async_copy(filt_ref, filt_held, sems.at[0])]
    copies.append(pltpu.make_async_copy(taps_ref, taps_held, sems.at[1]))
    for s in range(streams):
        source = x_ref.at[s, pl.ds(first, count)]
        copies.append(pltpu.make_async_copy(source, rows_ref.at[s], sems.at[2 + s]))
    if not late:
        copies.append(pltpu.make_async_copy(halo_ref, halo_held, sems.at[2 + streams]))
    for copy in copies:
        copy.start()
    copies[0].wait()

    @pl.loop(0, tiles)
    def _(tile):
        toeplitz(filt_held[tile], toep.at[tile])

    for copy in copies[1:]:
        copy.wait()

    @pl.loop(0, tiles)
    def _(tile):
        lanes = pl.ds(pl.multiple_of(tile * LANES, LANES), LANES)
        if late:
            rows = [rows_ref[s, :, lanes].astype(jnp.float32) for s in range(streams)]
            featured = [feature(rows[s], taps_held[s, :, lanes]) for s in range(streams)]
            gated = (featured[1] * featured[2])[16:].astype(jnp.bfloat16)
            query = featured[0][taps + 16 :]
            raw = [r[count - 8 :] for r in rows]
            raw.append(jnp.zeros_like(raw[0]))
            tail_ref[:taps, lanes] = gated[gated.shape[0] - taps :]
            tail_ref[taps:, lanes] = jnp.concatenate(raw, axis=0).astype(jnp.bfloat16)
        else:
            before = halo_held[taps:, lanes].astype(jnp.float32)
            featured = []
            for s in range(streams):
                rows = rows_ref[s, :, lanes].astype(jnp.float32)
                rows = jnp.concatenate([before[8 * s : 8 * s + 8], rows], axis=0)
                featured.append(feature(rows, taps_held[s, :, lanes])[8:])
            gated = (featured[1] * featured[2]).astype(jnp.bfloat16)
            gated = jnp.concatenate([halo_held[:taps, lanes], gated], axis=0)
            query = featured[0]
        for k, piece in enumerate(convolve(gated, query, groups, taps, toep.at[tile])):
            out_ref[k * taps : (k + 1) * taps, lanes] = piece


def local_part(x, halo, short_taps, long_filter):
    streams, tokens, channels = x.shape
    groups, taps = long_filter.shape
    filt = long_filter.reshape(channels // LANES, -1, taps)
    half, tail = tokens // 2, taps + 32
    late = halo is None
    shapes = [(half, channels), (tail, channels)] if late else [(half, channels)]
    return pl.pallas_call(
        functools.partial(local_kernel, late),
        in_specs=[pl.BlockSpec(memory_space=pl.ANY)] * 4,
        out_specs=[pl.BlockSpec(memory_space=pltpu.VMEM)] * len(shapes),
        out_shape=[jax.ShapeDtypeStruct(shape, jnp.bfloat16) for shape in shapes],
        scratch_shapes=[
            pltpu.VMEM((streams, half + taps + 16 if late else half, channels), jnp.bfloat16),
            pltpu.VMEM(short_taps.shape, jnp.float32),
            pltpu.VMEM(filt.shape, jnp.bfloat16),
            pltpu.VMEM((tail, channels), jnp.bfloat16),
            pltpu.VMEM((channels // LANES, groups * LANES // channels * taps, 2 * taps), jnp.bfloat16),
            pltpu.SemaphoreType.DMA((streams + 3,)),
        ],
        compiler_params=pltpu.CompilerParams(vmem_limit_bytes=VMEM),
        cost_estimate=pl.CostEstimate(flops=1 << 30, bytes_accessed=4 << 20, transcendentals=0),
        name="late_tokens" if late else "early_tokens",
    )(x, short_taps, filt, filt if late else halo)


def project_kernel(slots, side, outs, has_start, place_ref, *refs):
    total = sum(count for _, options in slots for _, count in options)
    x_refs, w_ref = refs[:total], refs[total]
    held, weight, acc, start, x_sems, w_sems, start_sem = refs[-7:]
    out_refs = refs[len(refs) - 7 - outs : len(refs) - 7]
    at, toward, th, u = [place_ref[i] for i in range(4)]
    parts, half, depth = held.shape[1:]
    per_zh = w_ref.shape[0]

    def fetch(slot, first, count, part):
        source = x_refs[first + part] if count > 1 else x_refs[first].at[pl.ds(part * half, half)]
        return pltpu.make_async_copy(source, held.at[slot, part], x_sems.at[slot, part])

    def rows(slot, y, z):
        return pltpu.make_async_copy(w_ref.at[y, :, z], weight.at[slot], w_sems.at[slot])

    @pl.when(u < WORKERS)
    def _():
        firsts = []
        position = 0
        for slot, (limit, options) in enumerate(slots):
            distance = options[0][0]
            if limit is not None:
                distance = jnp.where(u < limit, distance, options[1][0])
            block = jnp.clip(at + toward * distance, 0, LINE_LEN - 1)
            upper = jnp.where(block >= per_zh, 1, 0)
            column = th if side == 0 else 1 - th
            rows(slot, block - per_zh * upper, 2 * upper + column).start()
            firsts.append((position, options[0][1]))
            for option, (_, count) in enumerate(options):
                for part in range(parts):
                    copy = fetch(slot, position, count, part)
                    if limit is None:
                        copy.start()
                    else:
                        pl.when(u < limit if option == 0 else u >= limit)(copy.start)
                position += count
        if has_start:
            from_start = pltpu.make_async_copy(refs[total + 1], start, start_sem)
            from_start.start()

        for slot in range(len(slots)):
            rows(slot, 0, 0).wait()
            for part in range(parts):
                fetch(slot, *firsts[slot], part).wait()
            term = jnp.dot(
                held[slot].reshape(parts * half, depth),
                weight[slot].reshape(depth, weight.shape[-1]),
                preferred_element_type=jnp.float32,
            )
            if slot > 0:
                term = acc[...] + term
            if slot < len(slots) - 1:
                acc[...] = term
            else:
                if has_start:
                    from_start.wait()
                    term = start[...] + term
                for out_ref in out_refs:
                    out_ref[...] = term.astype(out_ref.dtype)


def project(slots, place, weights, side, start, kinds, name):
    half, depth = slots[0][1][0][1][0].shape
    ys, members, zs, rows, columns = weights.shape
    blocks, tokens = len(slots), 2 * half
    operands = [part for _, options in slots for _, block in options for part in block] + [weights]
    if start is not None:
        operands.append(start)
    shape_of_slots = tuple(
        (limit, tuple((distance, len(block)) for distance, block in options)) for limit, options in slots
    )
    return pl.pallas_call(
        functools.partial(project_kernel, shape_of_slots, side, len(kinds), start is not None),
        grid_spec=pltpu.PrefetchScalarGridSpec(
            num_scalar_prefetch=1,
            grid=(1,),
            in_specs=[pl.BlockSpec(memory_space=pl.ANY)] * len(operands),
            out_specs=[pl.BlockSpec((tokens, columns), lambda i, place: (0, 0))] * len(kinds),
            scratch_shapes=[
                pltpu.VMEM((blocks, 2, half, depth), jnp.bfloat16),
                pltpu.VMEM((blocks, members, rows, columns), jnp.bfloat16),
                pltpu.VMEM((tokens, columns), jnp.float32),
                pltpu.VMEM((tokens, columns) if start is not None else (8, LANES), jnp.float32),
                pltpu.SemaphoreType.DMA((blocks, 2)),
                pltpu.SemaphoreType.DMA((blocks,)),
                pltpu.SemaphoreType.DMA,
            ],
        ),
        out_shape=[jax.ShapeDtypeStruct((tokens, columns), kind) for kind in kinds],
        compiler_params=pltpu.CompilerParams(vmem_limit_bytes=VMEM),
        cost_estimate=pl.CostEstimate(
            flops=tokens * columns, bytes_accessed=tokens * columns, transcendentals=0
        ),
        name=name,
    )(place, *operands)


def per_device(projected, short_taps, long_filter, out_weight):
    core, at, th = lax.axis_index("c"), lax.axis_index(TP), lax.axis_index("th")
    u = jnp.where(core == 0, at, LINE_LEN - 1 - at)
    toward = jnp.where(core == 0, 1, -1)
    place = jnp.stack([at, toward, th, u]).astype(jnp.int32)
    in_order = lax.optimization_barrier

    late, tail = local_part(projected, None, short_taps, long_filter)
    next_seq = [(i, i + 1) for i in range(lax.axis_size(SEQ) - 1)]
    halo = lax.ppermute(tail, SEQ, next_seq)

    own_shard, place, _ = in_order((out_weight, place, late))
    shard = lax.all_gather(own_shard, ("zh", "th"), axis=0, tiled=True)
    projected, halo, shard = in_order((projected, halo, shard))
    weights = lax.all_gather(shard, PLANE, axis=0, tiled=True)
    projected, halo, _ = in_order((projected, halo, shard))
    (early,) = local_part(projected, halo, short_taps, long_filter)
    rows, columns = out_weight.shape
    parts = lax.axis_size(("zh", "th"))
    weights = weights.reshape(lax.axis_size("y"), -1, parts, rows, columns)

    came = [(early, late)]
    back = [(early, late)]
    for step in range(1, LINE_LEN - 2):
        before, behind = came[-1]
        before = inward(before, step)
        behind = inward(behind, step)
        came.append((before, behind))
        if step > 2:
            back.append(tuple(outward(part, step - 2) for part in back[-1]))

    kinds = (jnp.float32, jnp.bfloat16)
    near = [(None, [(d, came[d])]) for d in range(5)]
    (total,) = project(near, place, weights, 1, None, kinds[:1], "partner_near")
    fifth = came[5]
    came.append(tuple(inward(part, LINE_LEN - 2) for part in fifth))
    sixth, total, back[3] = in_order((came[6], total, back[3]))
    came.append(tuple(inward(part, LINE_LEN - 1) for part in sixth))
    far = [
        (3, [(5, fifth), (-3, back[3])]),
        (2, [(6, sixth), (-2, back[2])]),
        (None, [(-1, back[1])]),
    ]
    total, ready = project(far, place, weights, 1, total, kinds, "partner_far")
    sent_first = deliver(ready, (1, 2, 3))
    last, total = in_order((came[7], total))
    (ready,) = project([(None, [(7, last)])], place, weights, 1, total, kinds[1:], "partner_last")
    sent_last = deliver(ready, (0,))

    every = near + far[:2] + [(1, [(7, last), (-1, back[1])])]
    (mine,) = project(every, place, weights, 0, None, kinds[1:], "own_columns")
    given = jnp.where(u == WORKERS, sent_last, sent_first)
    return jnp.where(u < WORKERS, mine, given)


def solution(mesh):
    split = Mesh(mesh.devices.reshape(2, 4, 4, 2, 2, WORKERS), SEQ + TP)
    in_specs = (P(None, SEQ, TP), P(None, None, TP), P(TP, None), P(SEQ, TP))
    return jax.shard_map(
        per_device, mesh=split, in_specs=in_specs, out_specs=P(SEQ, TP), check_vma=False
    )
```

```python
import functools

import jax
import jax.numpy as jnp
from jax import lax
from jax.experimental import pallas as pl
from jax.experimental.pallas import tpu as pltpu
from jax.sharding import Mesh, PartitionSpec as P

SEQ = ("zh", "y", "x", "c")
PLANE = ("y", "x", "c")
TP = ("th", "tl")
LINE = ("c",) + TP
LANES = 128
LINE_LEN = 8
WORKERS = 4
VMEM = 60 << 20


def on_line(pairs):
    place = lambda u, core: core * LINE_LEN + (u if core == 0 else LINE_LEN - 1 - u)
    return [(place(a, core), place(b, core)) for core in (0, 1) for a, b in pairs]


def inward(block, step):
    return lax.ppermute(block, LINE, on_line([(u, u - 1) for u in range(1, LINE_LEN + 1 - step)]))


def outward(block, step):
    return lax.ppermute(block, LINE, on_line([(u, u + 1) for u in range(step - 1, WORKERS - 1)]))


def deliver(block, workers):
    return lax.ppermute(block, LINE, on_line([(u, u + WORKERS) for u in workers]))


def feature(rows, taps):
    return (
        taps[0:1] * rows
        + taps[1:2] * pltpu.roll(rows, 1, 0)
        + taps[2:3] * pltpu.roll(rows, 2, 0)
    )


def toeplitz(filt, toep):
    groups, taps = filt.shape
    lag = lax.broadcasted_iota(jnp.int32, (taps, 2 * taps), 0)
    col = lax.broadcasted_iota(jnp.int32, (taps, 2 * taps), 1)
    flip = jnp.where(lag + col == taps, 1.0, 0.0).astype(jnp.bfloat16)
    first = jnp.dot(filt, flip, preferred_element_type=jnp.float32)
    for g in range(groups):
        wide = jnp.broadcast_to(first[g : g + 1], (taps, 2 * taps))
        wide = pltpu.roll(wide, 0, 1, stride=1, stride_axis=0)
        toep[g * taps : (g + 1) * taps] = wide.astype(jnp.bfloat16)


def convolve(gated, query, groups, taps, toep):
    group_of = lax.broadcasted_iota(jnp.int32, (taps, 2 * LANES), 1) % LANES // (LANES // groups)
    pieces = []
    for pair in range(query.shape[0] // taps // 2):
        base = 2 * pair * taps
        window = jnp.concatenate(
            [gated[base : base + 2 * taps], gated[base + taps : base + 3 * taps]], axis=1
        )
        every = jnp.dot(toep[...], window, preferred_element_type=jnp.float32)
        conv = every[:taps]
        for g in range(1, groups):
            conv = jnp.where(group_of == g, every[g * taps : (g + 1) * taps], conv)
        for k in range(2):
            at = base + k * taps
            piece = conv[:, k * LANES : (k + 1) * LANES] * query[at : at + taps]
            pieces.append(piece.astype(jnp.bfloat16))
    return pieces


def local_kernel(late, x_ref, taps_ref, filt_ref, halo_ref, *refs):
    out_ref, tail_ref = refs[0], refs[1] if late else None
    rows_ref, taps_held, filt_held, halo_held, toep, sems = refs[-6:]
    streams, count = rows_ref.shape[:2]
    tiles, groups, taps = filt_held.shape
    first = x_ref.shape[1] - count if late else 0
    copies = [pltpu.make_async_copy(filt_ref, filt_held, sems.at[0])]
    copies.append(pltpu.make_async_copy(taps_ref, taps_held, sems.at[1]))
    for s in range(streams):
        source = x_ref.at[s, pl.ds(first, count)]
        copies.append(pltpu.make_async_copy(source, rows_ref.at[s], sems.at[2 + s]))
    if not late:
        copies.append(pltpu.make_async_copy(halo_ref, halo_held, sems.at[2 + streams]))
    for copy in copies:
        copy.start()
    copies[0].wait()

    @pl.loop(0, tiles)
    def _(tile):
        toeplitz(filt_held[tile], toep.at[tile])

    for copy in copies[1:]:
        copy.wait()

    @pl.loop(0, tiles)
    def _(tile):
        lanes = pl.ds(pl.multiple_of(tile * LANES, LANES), LANES)
        if late:
            rows = [rows_ref[s, :, lanes].astype(jnp.float32) for s in range(streams)]
            featured = [feature(rows[s], taps_held[s, :, lanes]) for s in range(streams)]
            gated = (featured[1] * featured[2])[16:].astype(jnp.bfloat16)
            query = featured[0][taps + 16 :]
            raw = [r[count - 8 :] for r in rows]
            raw.append(jnp.zeros_like(raw[0]))
            tail_ref[:taps, lanes] = gated[gated.shape[0] - taps :]
            tail_ref[taps:, lanes] = jnp.concatenate(raw, axis=0).astype(jnp.bfloat16)
        else:
            before = halo_held[taps:, lanes].astype(jnp.float32)
            featured = []
            for s in range(streams):
                rows = rows_ref[s, :, lanes].astype(jnp.float32)
                rows = jnp.concatenate([before[8 * s : 8 * s + 8], rows], axis=0)
                featured.append(feature(rows, taps_held[s, :, lanes])[8:])
            gated = (featured[1] * featured[2]).astype(jnp.bfloat16)
            gated = jnp.concatenate([halo_held[:taps, lanes], gated], axis=0)
            query = featured[0]
        for k, piece in enumerate(convolve(gated, query, groups, taps, toep.at[tile])):
            out_ref[k * taps : (k + 1) * taps, lanes] = piece


def local_part(x, halo, short_taps, long_filter):
    streams, tokens, channels = x.shape
    groups, taps = long_filter.shape
    filt = long_filter.reshape(channels // LANES, -1, taps)
    half, tail = tokens // 2, taps + 32
    late = halo is None
    shapes = [(half, channels), (tail, channels)] if late else [(half, channels)]
    return pl.pallas_call(
        functools.partial(local_kernel, late),
        in_specs=[pl.BlockSpec(memory_space=pl.ANY)] * 4,
        out_specs=[pl.BlockSpec(memory_space=pltpu.VMEM)] * len(shapes),
        out_shape=[jax.ShapeDtypeStruct(shape, jnp.bfloat16) for shape in shapes],
        scratch_shapes=[
            pltpu.VMEM((streams, half + taps + 16 if late else half, channels), jnp.bfloat16),
            pltpu.VMEM(short_taps.shape, jnp.float32),
            pltpu.VMEM(filt.shape, jnp.bfloat16),
            pltpu.VMEM((tail, channels), jnp.bfloat16),
            pltpu.VMEM((channels // LANES, groups * LANES // channels * taps, 2 * taps), jnp.bfloat16),
            pltpu.SemaphoreType.DMA((streams + 3,)),
        ],
        compiler_params=pltpu.CompilerParams(vmem_limit_bytes=VMEM),
        cost_estimate=pl.CostEstimate(flops=1 << 30, bytes_accessed=4 << 20, transcendentals=0),
        name="late_tokens" if late else "early_tokens",
    )(x, short_taps, filt, filt if late else halo)


def project_kernel(slots, side, outs, has_start, place_ref, *refs):
    total = sum(count for _, options in slots for _, count in options)
    x_refs, w_ref = refs[:total], refs[total]
    held, weight, acc, start, x_sems, w_sems, start_sem = refs[-7:]
    out_refs = refs[len(refs) - 7 - outs : len(refs) - 7]
    at, toward, th, u = [place_ref[i] for i in range(4)]
    parts, half, depth = held.shape[1:]
    per_zh = w_ref.shape[0]

    def fetch(slot, first, count, part):
        source = x_refs[first + part] if count > 1 else x_refs[first].at[pl.ds(part * half, half)]
        return pltpu.make_async_copy(source, held.at[slot, part], x_sems.at[slot, part])

    def rows(slot, y, z):
        return pltpu.make_async_copy(w_ref.at[y, :, z], weight.at[slot], w_sems.at[slot])

    @pl.when(u < WORKERS)
    def _():
        firsts = []
        position = 0
        for slot, (limit, options) in enumerate(slots):
            distance = options[0][0]
            if limit is not None:
                distance = jnp.where(u < limit, distance, options[1][0])
            block = jnp.clip(at + toward * distance, 0, LINE_LEN - 1)
            upper = jnp.where(block >= per_zh, 1, 0)
            column = th if side == 0 else 1 - th
            rows(slot, block - per_zh * upper, 2 * upper + column).start()
            firsts.append((position, options[0][1]))
            for option, (_, count) in enumerate(options):
                for part in range(parts):
                    copy = fetch(slot, position, count, part)
                    if limit is None:
                        copy.start()
                    else:
                        pl.when(u < limit if option == 0 else u >= limit)(copy.start)
                position += count
        if has_start:
            from_start = pltpu.make_async_copy(refs[total + 1], start, start_sem)
            from_start.start()

        for slot in range(len(slots)):
            rows(slot, 0, 0).wait()
            for part in range(parts):
                fetch(slot, *firsts[slot], part).wait()
            term = jnp.dot(
                held[slot].reshape(parts * half, depth),
                weight[slot].reshape(depth, weight.shape[-1]),
                preferred_element_type=jnp.float32,
            )
            if slot > 0:
                term = acc[...] + term
            if slot < len(slots) - 1:
                acc[...] = term
            else:
                if has_start:
                    from_start.wait()
                    term = start[...] + term
                for out_ref in out_refs:
                    out_ref[...] = term.astype(out_ref.dtype)


def project(slots, place, weights, side, start, kinds, name):
    half, depth = slots[0][1][0][1][0].shape
    ys, members, zs, rows, columns = weights.shape
    blocks, tokens = len(slots), 2 * half
    operands = [part for _, options in slots for _, block in options for part in block] + [weights]
    if start is not None:
        operands.append(start)
    shape_of_slots = tuple(
        (limit, tuple((distance, len(block)) for distance, block in options)) for limit, options in slots
    )
    return pl.pallas_call(
        functools.partial(project_kernel, shape_of_slots, side, len(kinds), start is not None),
        grid_spec=pltpu.PrefetchScalarGridSpec(
            num_scalar_prefetch=1,
            grid=(1,),
            in_specs=[pl.BlockSpec(memory_space=pl.ANY)] * len(operands),
            out_specs=[pl.BlockSpec((tokens, columns), lambda i, place: (0, 0))] * len(kinds),
            scratch_shapes=[
                pltpu.VMEM((blocks, 2, half, depth), jnp.bfloat16),
                pltpu.VMEM((blocks, members, rows, columns), jnp.bfloat16),
                pltpu.VMEM((tokens, columns), jnp.float32),
                pltpu.VMEM((tokens, columns) if start is not None else (8, LANES), jnp.float32),
                pltpu.SemaphoreType.DMA((blocks, 2)),
                pltpu.SemaphoreType.DMA((blocks,)),
                pltpu.SemaphoreType.DMA,
            ],
        ),
        out_shape=[jax.ShapeDtypeStruct((tokens, columns), kind) for kind in kinds],
        compiler_params=pltpu.CompilerParams(vmem_limit_bytes=VMEM),
        cost_estimate=pl.CostEstimate(
            flops=tokens * columns, bytes_accessed=tokens * columns, transcendentals=0
        ),
        name=name,
    )(place, *operands)


def per_device(projected, short_taps, long_filter, out_weight):
    core, at, th = lax.axis_index("c"), lax.axis_index(TP), lax.axis_index("th")
    u = jnp.where(core == 0, at, LINE_LEN - 1 - at)
    toward = jnp.where(core == 0, 1, -1)
    place = jnp.stack([at, toward, th, u]).astype(jnp.int32)
    in_order = lax.optimization_barrier

    late, tail = local_part(projected, None, short_taps, long_filter)
    next_seq = [(i, i + 1) for i in range(lax.axis_size(SEQ) - 1)]
    halo = lax.ppermute(tail, SEQ, next_seq)

    own_shard, place, _ = in_order((out_weight, place, late))
    shard = lax.all_gather(own_shard, ("zh", "th"), axis=0, tiled=True)
    projected, halo, shard = in_order((projected, halo, shard))
    weights = lax.all_gather(shard, PLANE, axis=0, tiled=True)
    projected, halo, _ = in_order((projected, halo, shard))
    (early,) = local_part(projected, halo, short_taps, long_filter)
    rows, columns = out_weight.shape
    parts = lax.axis_size(("zh", "th"))
    weights = weights.reshape(lax.axis_size("y"), -1, parts, rows, columns)

    came = [(early, late)]
    back = [(early, late)]
    for step in range(1, LINE_LEN - 2):
        before, behind = came[-1]
        before = inward(before, step)
        behind = inward(behind, step)
        came.append((before, behind))
        if step > 2:
            back.append(tuple(outward(part, step - 2) for part in back[-1]))

    kinds = (jnp.float32, jnp.bfloat16)
    near = [(None, [(d, came[d])]) for d in range(5)]
    (total,) = project(near, place, weights, 1, None, kinds[:1], "partner_near")
    fifth = came[5]
    came.append(tuple(inward(part, LINE_LEN - 2) for part in fifth))
    sixth, total, back[3] = in_order((came[6], total, back[3]))
    came.append(tuple(inward(part, LINE_LEN - 1) for part in sixth))
    far = [
        (3, [(5, fifth), (-3, back[3])]),
        (2, [(6, sixth), (-2, back[2])]),
        (None, [(-1, back[1])]),
    ]
    (ready,) = project(far, place, weights, 1, total, kinds[1:], "partner_far")
    sent_first = deliver(ready, (1, 2, 3))
    last, total, _ = in_order((came[7], total, ready))
    end = [(None, [(5, fifth)]), (None, [(6, sixth)]), (None, [(7, last)])]
    (ready,) = project(end, place, weights, 1, total, kinds[1:], "partner_last")
    sent_last = deliver(ready, (0,))

    every = near + far[:2] + [(1, [(7, last), (-1, back[1])])]
    (mine,) = project(every, place, weights, 0, None, kinds[1:], "own_columns")
    given = jnp.where(u == WORKERS, sent_last, sent_first)
    return jnp.where(u < WORKERS, mine, given)


def solution(mesh):
    split = Mesh(mesh.devices.reshape(2, 4, 4, 2, 2, WORKERS), SEQ + TP)
    in_specs = (P(None, SEQ, TP), P(None, None, TP), P(TP, None), P(SEQ, TP))
    return jax.shard_map(
        per_device, mesh=split, in_specs=in_specs, out_specs=P(SEQ, TP), check_vma=False
    )
```

```python
import functools

import jax
import jax.numpy as jnp
from jax import lax
from jax.experimental import pallas as pl
from jax.experimental.pallas import tpu as pltpu
from jax.sharding import Mesh, PartitionSpec as P

SEQ = ("zh", "y", "x", "c")
PLANE = ("y", "x", "c")
TP = ("th", "tl")
LINE = ("c",) + TP
LANES = 128
LINE_LEN = 8
WORKERS = 4
VMEM = 60 << 20


def on_line(pairs):
    place = lambda u, core: core * LINE_LEN + (u if core == 0 else LINE_LEN - 1 - u)
    return [(place(a, core), place(b, core)) for core in (0, 1) for a, b in pairs]


def inward(block, step):
    return lax.ppermute(block, LINE, on_line([(u, u - 1) for u in range(1, LINE_LEN + 1 - step)]))


def outward(block, step):
    return lax.ppermute(block, LINE, on_line([(u, u + 1) for u in range(step - 1, WORKERS - 1)]))


def deliver(block, workers):
    return lax.ppermute(block, LINE, on_line([(u, u + WORKERS) for u in workers]))


def feature(rows, taps):
    return (
        taps[0:1] * rows
        + taps[1:2] * pltpu.roll(rows, 1, 0)
        + taps[2:3] * pltpu.roll(rows, 2, 0)
    )


def toeplitz(filt, toep):
    groups, taps = filt.shape
    lag = lax.broadcasted_iota(jnp.int32, (taps, 2 * taps), 0)
    col = lax.broadcasted_iota(jnp.int32, (taps, 2 * taps), 1)
    flip = jnp.where(lag + col == taps, 1.0, 0.0).astype(jnp.bfloat16)
    first = jnp.dot(filt, flip, preferred_element_type=jnp.float32)
    for g in range(groups):
        wide = jnp.broadcast_to(first[g : g + 1], (taps, 2 * taps))
        wide = pltpu.roll(wide, 0, 1, stride=1, stride_axis=0)
        toep[g * taps : (g + 1) * taps] = wide.astype(jnp.bfloat16)


def convolve(gated, query, groups, taps, toep):
    group_of = lax.broadcasted_iota(jnp.int32, (taps, 2 * LANES), 1) % LANES // (LANES // groups)
    pieces = []
    for pair in range(query.shape[0] // taps // 2):
        base = 2 * pair * taps
        window = jnp.concatenate(
            [gated[base : base + 2 * taps], gated[base + taps : base + 3 * taps]], axis=1
        )
        every = jnp.dot(toep[...], window, preferred_element_type=jnp.float32)
        conv = every[:taps]
        for g in range(1, groups):
            conv = jnp.where(group_of == g, every[g * taps : (g + 1) * taps], conv)
        for k in range(2):
            at = base + k * taps
            piece = conv[:, k * LANES : (k + 1) * LANES] * query[at : at + taps]
            pieces.append(piece.astype(jnp.bfloat16))
    return pieces


def local_kernel(late, x_ref, taps_ref, filt_ref, halo_ref, *refs):
    out_ref, tail_ref = refs[0], refs[1] if late else None
    rows_ref, taps_held, filt_held, halo_held, toep, sems = refs[-6:]
    streams, count = rows_ref.shape[:2]
    tiles, groups, taps = filt_held.shape
    first = x_ref.shape[1] - count if late else 0
    copies = [pltpu.make_async_copy(filt_ref, filt_held, sems.at[0])]
    copies.append(pltpu.make_async_copy(taps_ref, taps_held, sems.at[1]))
    for s in range(streams):
        source = x_ref.at[s, pl.ds(first, count)]
        copies.append(pltpu.make_async_copy(source, rows_ref.at[s], sems.at[2 + s]))
    if not late:
        copies.append(pltpu.make_async_copy(halo_ref, halo_held, sems.at[2 + streams]))
    for copy in copies:
        copy.start()
    copies[0].wait()

    @pl.loop(0, tiles)
    def _(tile):
        toeplitz(filt_held[tile], toep.at[tile])

    for copy in copies[1:]:
        copy.wait()

    @pl.loop(0, tiles)
    def _(tile):
        lanes = pl.ds(pl.multiple_of(tile * LANES, LANES), LANES)
        if late:
            rows = [rows_ref[s, :, lanes].astype(jnp.float32) for s in range(streams)]
            featured = [feature(rows[s], taps_held[s, :, lanes]) for s in range(streams)]
            gated = (featured[1] * featured[2])[16:].astype(jnp.bfloat16)
            query = featured[0][taps + 16 :]
            raw = [r[count - 8 :] for r in rows]
            raw.append(jnp.zeros_like(raw[0]))
            tail_ref[:taps, lanes] = gated[gated.shape[0] - taps :]
            tail_ref[taps:, lanes] = jnp.concatenate(raw, axis=0).astype(jnp.bfloat16)
        else:
            before = halo_held[taps:, lanes].astype(jnp.float32)
            featured = []
            for s in range(streams):
                rows = rows_ref[s, :, lanes].astype(jnp.float32)
                rows = jnp.concatenate([before[8 * s : 8 * s + 8], rows], axis=0)
                featured.append(feature(rows, taps_held[s, :, lanes])[8:])
            gated = (featured[1] * featured[2]).astype(jnp.bfloat16)
            gated = jnp.concatenate([halo_held[:taps, lanes], gated], axis=0)
            query = featured[0]
        for k, piece in enumerate(convolve(gated, query, groups, taps, toep.at[tile])):
            out_ref[k * taps : (k + 1) * taps, lanes] = piece


def local_part(x, halo, short_taps, long_filter):
    streams, tokens, channels = x.shape
    groups, taps = long_filter.shape
    filt = long_filter.reshape(channels // LANES, -1, taps)
    half, tail = tokens // 2, taps + 32
    late = halo is None
    shapes = [(half, channels), (tail, channels)] if late else [(half, channels)]
    return pl.pallas_call(
        functools.partial(local_kernel, late),
        in_specs=[pl.BlockSpec(memory_space=pl.ANY)] * 4,
        out_specs=[pl.BlockSpec(memory_space=pltpu.VMEM)] * len(shapes),
        out_shape=[jax.ShapeDtypeStruct(shape, jnp.bfloat16) for shape in shapes],
        scratch_shapes=[
            pltpu.VMEM((streams, half + taps + 16 if late else half, channels), jnp.bfloat16),
            pltpu.VMEM(short_taps.shape, jnp.float32),
            pltpu.VMEM(filt.shape, jnp.bfloat16),
            pltpu.VMEM((tail, channels), jnp.bfloat16),
            pltpu.VMEM((channels // LANES, groups * LANES // channels * taps, 2 * taps), jnp.bfloat16),
            pltpu.SemaphoreType.DMA((streams + 3,)),
        ],
        compiler_params=pltpu.CompilerParams(vmem_limit_bytes=VMEM),
        cost_estimate=pl.CostEstimate(flops=1 << 30, bytes_accessed=4 << 20, transcendentals=0),
        name="late_tokens" if late else "early_tokens",
    )(x, short_taps, filt, filt if late else halo)


def project_kernel(slots, side, outs, has_start, place_ref, *refs):
    total = sum(count for _, options in slots for _, count in options)
    x_refs, w_ref = refs[:total], refs[total]
    held, weight, acc, start, x_sems, w_sems, start_sem = refs[-7:]
    out_refs = refs[len(refs) - 7 - outs : len(refs) - 7]
    at, toward, th, u = [place_ref[i] for i in range(4)]
    parts, half, depth = held.shape[1:]
    per_zh = w_ref.shape[0]

    def fetch(slot, first, count, part):
        source = x_refs[first + part] if count > 1 else x_refs[first].at[pl.ds(part * half, half)]
        return pltpu.make_async_copy(source, held.at[slot, part], x_sems.at[slot, part])

    def rows(slot, y, z):
        return pltpu.make_async_copy(w_ref.at[y, :, z], weight.at[slot], w_sems.at[slot])

    @pl.when(u < WORKERS)
    def _():
        firsts = []
        position = 0
        for slot, (limit, options) in enumerate(slots):
            distance = options[0][0]
            if limit is not None:
                distance = jnp.where(u < limit, distance, options[1][0])
            block = jnp.clip(at + toward * distance, 0, LINE_LEN - 1)
            upper = jnp.where(block >= per_zh, 1, 0)
            column = th if side == 0 else 1 - th
            rows(slot, block - per_zh * upper, 2 * upper + column).start()
            firsts.append((position, options[0][1]))
            for option, (_, count) in enumerate(options):
                for part in range(parts):
                    copy = fetch(slot, position, count, part)
                    if limit is None:
                        copy.start()
                    else:
                        pl.when(u < limit if option == 0 else u >= limit)(copy.start)
                position += count
        if has_start:
            from_start = pltpu.make_async_copy(refs[total + 1], start, start_sem)
            from_start.start()

        for slot in range(len(slots)):
            rows(slot, 0, 0).wait()
            for part in range(parts):
                fetch(slot, *firsts[slot], part).wait()
            term = jnp.dot(
                held[slot].reshape(parts * half, depth),
                weight[slot].reshape(depth, weight.shape[-1]),
                preferred_element_type=jnp.float32,
            )
            if slot > 0:
                term = acc[...] + term
            if slot < len(slots) - 1:
                acc[...] = term
            else:
                if has_start:
                    from_start.wait()
                    term = start[...] + term
                for out_ref in out_refs:
                    out_ref[...] = term.astype(out_ref.dtype)


def project(slots, place, weights, side, start, kinds, name):
    half, depth = slots[0][1][0][1][0].shape
    ys, members, zs, rows, columns = weights.shape
    blocks, tokens = len(slots), 2 * half
    operands = [part for _, options in slots for _, block in options for part in block] + [weights]
    if start is not None:
        operands.append(start)
    shape_of_slots = tuple(
        (limit, tuple((distance, len(block)) for distance, block in options)) for limit, options in slots
    )
    return pl.pallas_call(
        functools.partial(project_kernel, shape_of_slots, side, len(kinds), start is not None),
        grid_spec=pltpu.PrefetchScalarGridSpec(
            num_scalar_prefetch=1,
            grid=(1,),
            in_specs=[pl.BlockSpec(memory_space=pl.ANY)] * len(operands),
            out_specs=[pl.BlockSpec((tokens, columns), lambda i, place: (0, 0))] * len(kinds),
            scratch_shapes=[
                pltpu.VMEM((blocks, 2, half, depth), jnp.bfloat16),
                pltpu.VMEM((blocks, members, rows, columns), jnp.bfloat16),
                pltpu.VMEM((tokens, columns), jnp.float32),
                pltpu.VMEM((tokens, columns) if start is not None else (8, LANES), jnp.float32),
                pltpu.SemaphoreType.DMA((blocks, 2)),
                pltpu.SemaphoreType.DMA((blocks,)),
                pltpu.SemaphoreType.DMA,
            ],
        ),
        out_shape=[jax.ShapeDtypeStruct((tokens, columns), kind) for kind in kinds],
        compiler_params=pltpu.CompilerParams(vmem_limit_bytes=VMEM),
        cost_estimate=pl.CostEstimate(
            flops=tokens * columns, bytes_accessed=tokens * columns, transcendentals=0
        ),
        name=name,
    )(place, *operands)


def per_device(projected, short_taps, long_filter, out_weight):
    core, at, th = lax.axis_index("c"), lax.axis_index(TP), lax.axis_index("th")
    u = jnp.where(core == 0, at, LINE_LEN - 1 - at)
    toward = jnp.where(core == 0, 1, -1)
    place = jnp.stack([at, toward, th, u]).astype(jnp.int32)
    in_order = lax.optimization_barrier

    late, tail = local_part(projected, None, short_taps, long_filter)
    next_seq = [(i, i + 1) for i in range(lax.axis_size(SEQ) - 1)]
    halo = lax.ppermute(tail, SEQ, next_seq)

    own_shard, place, _ = in_order((out_weight, place, late))
    shard = lax.all_gather(own_shard, ("zh", "th"), axis=0, tiled=True)
    projected, halo, shard = in_order((projected, halo, shard))
    weights = lax.all_gather(shard, PLANE, axis=0, tiled=True)
    projected, halo, _ = in_order((projected, halo, shard))
    (early,) = local_part(projected, halo, short_taps, long_filter)
    rows, columns = out_weight.shape
    parts = lax.axis_size(("zh", "th"))
    weights = weights.reshape(lax.axis_size("y"), -1, parts, rows, columns)

    came = [(early, late)]
    back = [(early, late)]
    for step in range(1, LINE_LEN - 2):
        before, behind = came[-1]
        before = inward(before, step)
        behind = inward(behind, step)
        came.append((before, behind))
        if step > 2:
            back.append(tuple(outward(part, step - 2) for part in back[-1]))

    kinds = (jnp.float32, jnp.bfloat16)
    near = [(None, [(d, came[d])]) for d in range(5)] + [(3, [(5, came[5]), (-3, back[3])])]
    came.append(tuple(inward(part, LINE_LEN - 2) for part in came[5]))
    slots = near + [(None, [(-2, back[2])]), (None, [(-1, back[1])])]
    total, ready = project(slots, place, weights, 1, None, kinds, "partner_first")
    sent_first = deliver(ready, (2, 3))
    sixth, total = in_order((came[6], total))
    came.append(tuple(inward(part, LINE_LEN - 1) for part in sixth))
    last, total = in_order((came[7], total))
    slots = [(None, [(6, sixth)]), (None, [(7, last)])]
    (ready,) = project(slots, place, weights, 1, total, kinds[1:], "partner_last")
    sent_last = deliver(ready, (0, 1))

    every = near + [(2, [(6, sixth), (-2, back[2])]), (1, [(7, last), (-1, back[1])])]
    (mine,) = project(every, place, weights, 0, None, kinds[1:], "own_columns")
    given = jnp.where(u < WORKERS + 2, sent_last, sent_first)
    return jnp.where(u < WORKERS, mine, given)


def solution(mesh):
    split = Mesh(mesh.devices.reshape(2, 4, 4, 2, 2, WORKERS), SEQ + TP)
    in_specs = (P(None, SEQ, TP), P(None, None, TP), P(TP, None), P(SEQ, TP))
    return jax.shard_map(
        per_device, mesh=split, in_specs=in_specs, out_specs=P(SEQ, TP), check_vma=False
    )
```
